512 devices in a mesh: stream: 16 (over z, core), span: 32 (over x, y).
Axes of the slice: x: 4, y: 8, z: 8, core: 2. Of those that a mesh axis runs over, the one named last changes fastest.
Arguments:
- right_side: bfloat16 [16, 1792, 1600], P('stream', 'span'), may hold values from -2.390625 to 2.390625
- up_blocks: bfloat16 [16, 1792, 20000], P('stream', 'span'), may hold values from -0.375 to 0.375
- inverses: bfloat16 [16, 1792, 10000], P('stream', 'span'), may hold values from -0.625 to 0.625
- up_cells: int32 [16, 1792, 2], P('stream', 'span'), may hold values from 0 to 27
- piece_rhs: bfloat16 [16, 1536, 1600], P('stream', 'span'), may hold values from -2.390625 to 2.390625
- piece_blocks: bfloat16 [16, 1536, 10000], P('stream', 'span'), may hold values from -0.375 to 0.375
- piece_up: int32 [16, 1536], P('stream', 'span'), may hold values from 0 to 27
- piece_owner: int32 [16, 1536, 1], P('stream', 'span'), may hold values from 0 to 31; in each aligned block of 24 rows (0 to 23, 24 to 47, ..., all dimensions but the last counted through in order) at most 2 rows name the same one
- piece_cell: int32 [16, 1536], P('stream', 'span'), may hold values from 0 to 27
Outputs:
- sweep_states: bfloat16 [16, 1792, 1600], P('stream', 'span')
The draws below stay inside these ranges and needn't reach their ends.
Inputs may be any that keep to these rules, and one draw needn't show every extreme that they name: `up_cells`: each upstream cell is on the device of the same span index in the previous section and in the same sweep group. `piece_up`: the upstream cell of a piece is on the device of the same span index in the previous section and in the piece's sweep group. `piece_owner`: among the rows of one device in one sweep group (aligned blocks of 24 rows), at most 2 name the same owner device; some device and group reach 2. `piece_cell`: the owner cell is in the piece's sweep group on the owner device.
All inputs are finite; a program needn't handle non-finite values.
Results may differ from the reference program's by a relative error of at most 0.035.
Values may be sent and summed in bfloat16 or wider, within the bound.
A program may use at most 64 MiB of HBM per device.

```python
import math
import jax
import jax.numpy as jnp
import numpy as np

U = 100
R = 16
CELLS = 56
SLOTS = 48
CELL_GRP = 28
SLOTS_GRP = 24
CAP = 2
SECTIONS = 16
SEC_CELLS = 1792
SEC_SLOTS = 1536
N_SPAN = 32


def set_ends(entries, own_key, least, top_value):
    longest = entries.shape.index(max(entries.shape))
    spots = []
    for shift in (0, 1):
        where = [jax.random.randint(jax.random.fold_in(own_key, axis), (), 0, length) for axis, length in enumerate(entries.shape)]
        where[longest] = (where[longest] + shift) % entries.shape[longest]
        spots.append(tuple(where))
    return entries.at[spots[0]].set(least).at[spots[1]].set(top_value)


def steps_of(stream_key, extent, split, low, top_value):
    gain = 1.0
    for dim, blocks in split:
        draws = jax.random.uniform(jax.random.fold_in(jax.random.fold_in(stream_key, 6), dim), (blocks,), jnp.float32, low / len(split), top_value / len(split))
        gain = gain * jnp.repeat(jnp.exp(draws), extent[dim] // blocks).reshape((-1,) + (1,) * (len(extent) - 1 - dim))
    return gain


def assign_block(own_key, own, number, rows, number_of, top, bound, lean):
    sequence = jax.random.permutation(own_key, number_of)
    crowded, common = portions_of(number_of, rows * top, bound, lean, True), portions_of(number_of, rows * top, bound, lean, False)
    places = jnp.arange(number_of)

    def named(sizes, turn):
        used = int((sizes > 0).sum())
        fixed = max(1, used // 4)
        moved = fixed + (places - fixed + turn * (used - fixed)) % max(1, number_of - fixed)
        return jnp.zeros((number_of,), jnp.int32).at[sequence[jnp.where(places < fixed, places, moved)]].set(jnp.asarray(sizes, jnp.int32))

    sizes = jnp.where(number % 4 == 0, named(crowded, number // 4), named(common, number - number // 4 - 1))
    mixed = jax.random.permutation(jax.random.fold_in(own, 3), number_of)
    giver, taker = mixed[0:number_of // 2 * 2:2], mixed[1:number_of // 2 * 2:2]
    slack = jnp.minimum(sizes[giver] - 1, bound - sizes[taker]) // 2
    slack = jnp.where((giver == sequence[0]) | (taker == sequence[0]) | (sizes[taker] == 0), 0, jnp.maximum(slack, 0))
    moved = jax.random.randint(jax.random.fold_in(own, 4), (number_of // 2,), 0, 1 << 20) % (slack + 1)
    sizes = sizes.at[giver].add(-moved).at[taker].add(moved)
    items = jnp.searchsorted(jnp.cumsum(sizes), jnp.arange(rows * top), side="right").astype(jnp.int32)
    listing = items.reshape(top, rows).T
    listing = listing[jax.random.permutation(jax.random.fold_in(own, 1), rows)]
    turn = jax.random.randint(jax.random.fold_in(own, 2), (rows, 1), 0, top)
    return jnp.take_along_axis(listing, (jnp.arange(top)[None, :] + turn) % top, axis=1)


def portions_of(count, total, reach, skew, full):
    weights = [(1 << 20) // math.isqrt(grade ** skew) + 1 for grade in range(1, count + 1)]
    largest = reach if full else min(reach, max(-(-total // count), total * weights[0] // sum(weights)))
    least = 1 if total - largest >= count - 1 else 0
    holding, surplus = [largest] + [least] * (count - 1), total - largest - least * (count - 1)
    while surplus > 0:
        candidates = [i for i in range(1, count) if holding[i] < largest] or [i for i in range(1, count) if holding[i] < reach]
        pool, left = sum([weights[i] for i in candidates]), surplus
        for i in candidates:
            more = min(reach - holding[i], max(1, left * weights[i] // pool), surplus)
            holding[i] = holding[i] + more
            surplus = surplus - more
    return np.array(holding)


def normal_values(rng, dims, width, limit, pieces=(), kind=jnp.bfloat16):
    level = steps_of(rng, dims, pieces, -0.22, 0.18) if pieces else 1.0
    entries = jax.random.normal(rng, dims, jnp.float32) * width * level
    return jnp.minimum(jnp.maximum(entries, -limit), limit).astype(kind)


def setup_inputs(seed: int = 0) -> dict:
    splits = jax.random.split(jax.random.key(seed), 10)
    right_side = normal_values(splits[0], (SECTIONS, SEC_CELLS, U * R), 0.4, 2.390625, ((0, 16), (1, 32)))
    up_blocks = normal_values(splits[1], (SECTIONS, SEC_CELLS, 2 * U * U), (3 * U) ** -0.5, 0.375, ((0, 16), (1, 32)))
    inverses = normal_values(splits[2], (SECTIONS, SEC_CELLS, U * U), U ** -0.5, 0.625, ((0, 16), (1, 32)))
    up_cells = set_ends(jax.random.randint(splits[3], (SECTIONS, SEC_CELLS, 2), 0, CELL_GRP), jax.random.fold_in(splits[3], 1), 0, CELL_GRP - 1).astype(jnp.int32)
    piece_rhs = normal_values(splits[4], (SECTIONS, SEC_SLOTS, U * R), 0.4, 2.390625, ((0, 16), (1, 32)))
    piece_blocks = normal_values(splits[5], (SECTIONS, SEC_SLOTS, U * U), (3 * U) ** -0.5, 0.375, ((0, 16), (1, 32)))
    piece_up = set_ends(jax.random.randint(splits[6], (SECTIONS, SEC_SLOTS), 0, CELL_GRP), jax.random.fold_in(splits[6], 1), 0, CELL_GRP - 1).astype(jnp.int32)
    piece_owner_keys = jax.random.split(jax.random.fold_in(splits[7], 1), SECTIONS * SEC_SLOTS // SLOTS_GRP)
    piece_owner_turns = jax.random.permutation(jax.random.fold_in(splits[7], 3), SECTIONS * SEC_SLOTS // SLOTS_GRP)
    piece_owner = jax.vmap(lambda own, number: assign_block(jax.random.fold_in(splits[7], 2), own, number, SLOTS_GRP, N_SPAN, 1, CAP, 2))(piece_owner_keys, piece_owner_turns).reshape((SECTIONS, SEC_SLOTS, 1))
    piece_cell = set_ends(jax.random.randint(splits[8], (SECTIONS, SEC_SLOTS), 0, CELL_GRP), jax.random.fold_in(splits[8], 1), 0, CELL_GRP - 1).astype(jnp.int32)
    return {"right_side": right_side, "up_blocks": up_blocks, "inverses": inverses, "up_cells": up_cells, "piece_rhs": piece_rhs, "piece_blocks": piece_blocks, "piece_up": piece_up, "piece_owner": piece_owner, "piece_cell": piece_cell}


def reference(right_side, up_blocks, inverses, up_cells, piece_rhs, piece_blocks, piece_up, piece_owner, piece_cell):
    cell_ids = jnp.arange(SEC_CELLS, dtype=jnp.int32)
    cell_base = (cell_ids // CELLS) * CELLS + ((cell_ids % CELLS) // CELL_GRP) * CELL_GRP
    piece_ids = jnp.arange(SEC_SLOTS, dtype=jnp.int32)
    piece_base = (piece_ids // SLOTS) * CELLS + ((piece_ids % SLOTS) // SLOTS_GRP) * CELL_GRP
    upstream = jnp.zeros((SEC_CELLS, U, R), jnp.bfloat16)
    results = []
    for section in range(SECTIONS):
        nearby = upstream[(cell_base[:, None] + up_cells[section]).astype(jnp.int32)].astype(jnp.float32)
        blocks = up_blocks[section].reshape(SEC_CELLS, 2, U, U).astype(jnp.float32)
        owned = right_side[section].reshape(SEC_CELLS, U, R).astype(jnp.float32) - jnp.einsum("nkij,nkjr->nir", blocks, nearby)
        piece_near = upstream[(piece_base + piece_up[section]).astype(jnp.int32)].astype(jnp.float32)
        piece_mats = piece_blocks[section].reshape(SEC_SLOTS, U, U).astype(jnp.float32)
        partial_value = (piece_rhs[section].reshape(SEC_SLOTS, U, R).astype(jnp.float32) - jnp.einsum("nij,njr->nir", piece_mats, piece_near)).astype(jnp.bfloat16)
        owners = (piece_owner[section, :, 0] * CELLS + piece_base - (piece_ids // SLOTS) * CELLS + piece_cell[section]).astype(jnp.int32)
        summed = jax.ops.segment_sum(partial_value.astype(jnp.float32), owners, num_segments=SEC_CELLS)
        merged = (owned + summed).astype(jnp.bfloat16)
        inverse_blocks = inverses[section].reshape(SEC_CELLS, U, U).astype(jnp.float32)
        solved = jnp.einsum("nij,njr->nir", inverse_blocks, merged.astype(jnp.float32)).astype(jnp.bfloat16)
        results.append(solved.reshape(SEC_CELLS, U * R))
        upstream = solved
    return jnp.stack(results)
```

```python
import functools

import jax
import jax.numpy as jnp
from jax import lax
from jax.experimental import pallas as pl
from jax.experimental.pallas import tpu as pltpu
from jax.sharding import PartitionSpec as P

U = 100
R = 16
LANES = 128
GROUPS = 2
CAP = 2
MSG = CAP * R
BLOCK = 4
MESH = pl.DeviceIdType.MESH


def times_transposed(states, block):
    return lax.dot_general(
        states, block, (((1,), (1,)), ((), ())), preferred_element_type=jnp.float32
    )


def section_kernel(
    sizes,
    up_cells,
    piece_up,
    owner_row,
    cell_row,
    right_side,
    piece_rhs,
    up_blocks,
    inverses,
    piece_blocks,
    out,
    face_pad,
    inverse_pad,
    piece_pad,
    rhs_pad,
    piece_rhs_pad,
    table,
    slot_table,
    index_out,
    index_in,
    selector,
    outbox,
    inbox,
    arrived_0,
    arrived_1,
    sent,
    owned,
    table_sem,
    index_sems,
    outbox_sems,
    inbox_sems,
    sent_sems,
    arrived_sems,
):
    sections, span_x, span_y, cells, slots = sizes
    span = span_x * span_y
    cell_grp, slot_grp = cells // GROUPS, slots // GROUPS
    section = lax.axis_index("stream")
    me = lax.axis_index("span")
    me_x, me_y = me // span_y, me % span_y

    def peer(turn):
        x = (me_x + turn // span_y) % span_x
        y = (me_y + turn % span_y) % span_y
        return x * span_y + y

    arrived = (arrived_0, arrived_1)
    barrier = pltpu.get_barrier_semaphore()

    @pl.loop(1, span)
    def _(turn):
        pl.semaphore_signal(barrier, inc=1, device_id={"span": peer(turn)}, device_id_type=MESH)

    for step in (1, sections - 1):
        pl.semaphore_signal(
            barrier, inc=1, device_id={"stream": (section + step) % sections}, device_id_type=MESH
        )

    turn_col = lax.broadcasted_iota(jnp.int32, (span, slots), 0)
    slot_lane = lax.broadcasted_iota(jnp.int32, (span, slots), 1)
    match = owner_row[...] == peer(turn_col)
    lane = lax.broadcasted_iota(jnp.int32, (span, LANES), 1)
    mine = lane // MSG == lax.broadcasted_iota(jnp.int32, (span, LANES), 0) % BLOCK
    slot_values = jnp.zeros((span, LANES), jnp.int32)
    for group in range(GROUPS):
        indices = jnp.zeros((span, LANES), jnp.int32)
        named = match & (slot_lane // slot_grp == group)
        lowest = jnp.min(jnp.where(named, slot_lane, slots), axis=1, keepdims=True)
        highest = jnp.max(jnp.where(named, slot_lane, -1), axis=1, keepdims=True)
        found = (highest >= lowest, highest > lowest)
        for place, piece in enumerate((lowest, highest)):
            chosen = (slot_lane == piece) & found[place]
            piece = jnp.where(found[place], piece, group * slot_grp)
            target = jnp.sum(jnp.where(chosen, cell_row[...] + 1, 0), axis=1, keepdims=True)
            slot_values = jnp.where(
                lane == group * CAP + place, piece, slot_values
            )
            indices = jnp.where(mine & (lane // R % CAP == place), target, indices)
        index_out[:, group, :] = indices
    table[...] = slot_values
    to_slots = pltpu.make_async_copy(table, slot_table, table_sem)
    to_slots.start()

    def padded(source, target, count):
        target[...] = jnp.zeros_like(target)

        @pl.loop(0, count)
        def _(i):
            target[i, : source.shape[1], : source.shape[2]] = source[i]

    padded(right_side, rhs_pad, cells)
    padded(piece_rhs, piece_rhs_pad, slots)

    to_slots.wait()
    pl.semaphore_wait(barrier, span + 1)

    index_in[0] = index_out[0]

    @pl.loop(1, span)
    def _(turn):
        pltpu.make_async_remote_copy(
            src_ref=index_out.at[turn],
            dst_ref=index_in.at[turn],
            send_sem=index_sems.at[0],
            recv_sem=index_sems.at[1],
            device_id={"span": peer(turn)},
            device_id_type=MESH,
        ).start()

    padded(piece_blocks, piece_pad, slots)
    padded(up_blocks, face_pad, 2 * cells)
    padded(inverses, inverse_pad, cells)

    remote = pl.ds(1, span - 1)
    pltpu.make_async_copy(index_in.at[remote], index_in.at[remote], index_sems.at[1]).wait()
    row = lax.broadcasted_iota(jnp.int32, (cell_grp * R, LANES), 0)
    column = lax.broadcasted_iota(jnp.int32, (cell_grp * R, LANES), 1)
    same_side = row % R == column % R
    for group in range(GROUPS):
        for part in range(span // BLOCK):
            named = index_in[BLOCK * part, pl.ds(group, 1), :]
            for j in range(1, BLOCK):
                named = named + index_in[BLOCK * part + j, pl.ds(group, 1), :]
            hit = same_side & (row // R + 1 == named)
            selector[group, :, pl.ds(part * LANES, LANES)] = hit.astype(jnp.bfloat16)

    def start_group(group):
        @pl.when(section == 0)
        def _():
            arrived[group][...] = jnp.zeros_like(arrived[group])

        @pl.when(section > 0)
        def _():
            pltpu.make_async_copy(
                arrived[group], arrived[group], arrived_sems.at[group]
            ).wait()

        def part(index, own_first):
            for j in range(BLOCK):
                turn = index * BLOCK + j
                for place in range(CAP):
                    piece = slot_table[turn, group * CAP + place]
                    near = arrived[group][piece_up[piece]]
                    term = piece_rhs_pad[piece].astype(jnp.float32) - times_transposed(
                        near, piece_pad[piece]
                    )
                    term = term.astype(jnp.bfloat16)
                    if own_first and j == 0:
                        inbox[group, 0, pl.ds(place * R, R), :] = term
                    else:
                        outbox[group, turn, pl.ds(place * R, R), :] = term
            for j in range(1 if own_first else 0, BLOCK):
                turn = index * BLOCK + j
                pltpu.make_async_remote_copy(
                    src_ref=outbox.at[group, turn],
                    dst_ref=inbox.at[group, turn],
                    send_sem=outbox_sems.at[group],
                    recv_sem=inbox_sems.at[group],
                    device_id={"span": peer(turn)},
                    device_id_type=MESH,
                ).start()

        @pl.loop(1, span // BLOCK)
        def _(index):
            part(index, False)

        part(0, True)

        @pl.loop(0, cell_grp // BLOCK)
        def _(index):
            for j in range(BLOCK):
                cell = index * BLOCK + j
                whole = group * cell_grp + cell
                total = rhs_pad[whole].astype(jnp.float32)
                for face in range(2):
                    near = arrived[group][up_cells[whole, face]]
                    total = total - times_transposed(near, face_pad[2 * whole + face])
                owned[group, cell] = total

    def finish_group(group):
        pltpu.make_async_copy(
            inbox.at[group, remote], inbox.at[group, remote], inbox_sems.at[group]
        ).wait()
        messages = inbox[group].reshape(span * MSG, LANES)
        summed = jnp.dot(selector[group], messages, preferred_element_type=jnp.float32)
        owned[group] = owned[group] + summed.reshape(cell_grp, R, LANES)

        @pl.loop(0, cell_grp // BLOCK)
        def _(index):
            for j in range(BLOCK):
                cell = index * BLOCK + j
                whole = group * cell_grp + cell
                merged = owned[group, cell].astype(jnp.bfloat16)
                sent[group, cell] = times_transposed(merged, inverse_pad[whole]).astype(
                    jnp.bfloat16
                )

        @pl.when(section < sections - 1)
        def _():
            downstream(group).start()

        out[pl.ds(group * cell_grp, cell_grp)] = sent[group, :, :, :U]

    def downstream(group):
        return pltpu.make_async_remote_copy(
            src_ref=sent.at[group],
            dst_ref=arrived[group],
            send_sem=sent_sems.at[group],
            recv_sem=arrived_sems.at[group],
            device_id={"stream": (section + 1) % sections},
            device_id_type=MESH,
        )

    for group in range(GROUPS):
        start_group(group)
    for group in range(GROUPS):
        finish_group(group)

    pltpu.make_async_copy(index_out.at[remote], index_out.at[remote], index_sems.at[0]).wait()
    for group in range(GROUPS):
        pltpu.make_async_copy(
            outbox.at[group, remote], outbox.at[group, remote], outbox_sems.at[group]
        ).wait()

        @pl.when(section < sections - 1)
        def _():
            downstream(group).wait_send()


def on_device(
    sizes,
    right_side,
    up_blocks,
    inverses,
    up_cells,
    piece_rhs,
    piece_blocks,
    piece_up,
    piece_owner,
    piece_cell,
):
    sections, span_x, span_y, cells, slots = sizes
    span = span_x * span_y
    cell_grp = cells // GROUPS
    vmem = pl.BlockSpec(memory_space=pltpu.VMEM)
    smem = pl.BlockSpec(memory_space=pltpu.SMEM)
    bf16 = jnp.bfloat16
    states = pl.pallas_call(
        functools.partial(section_kernel, sizes),
        out_shape=jax.ShapeDtypeStruct((cells, R, U), bf16),
        in_specs=[smem, smem] + [vmem] * 7,
        out_specs=vmem,
        scratch_shapes=[
            pltpu.VMEM((2 * cells, LANES, LANES), bf16),
            pltpu.VMEM((cells, LANES, LANES), bf16),
            pltpu.VMEM((slots, LANES, LANES), bf16),
            pltpu.VMEM((cells, R, LANES), bf16),
            pltpu.VMEM((slots, R, LANES), bf16),
            pltpu.VMEM((span, LANES), jnp.int32),
            pltpu.SMEM((span, LANES), jnp.int32),
            pltpu.VMEM((span, GROUPS, LANES), jnp.int32),
            pltpu.VMEM((span, GROUPS, LANES), jnp.int32),
            pltpu.VMEM((GROUPS, cell_grp * R, span * MSG), bf16),
            pltpu.VMEM((GROUPS, span, MSG, LANES), bf16),
            pltpu.VMEM((GROUPS, span, MSG, LANES), bf16),
            pltpu.VMEM((cell_grp, R, LANES), bf16),
            pltpu.VMEM((cell_grp, R, LANES), bf16),
            pltpu.VMEM((GROUPS, cell_grp, R, LANES), bf16),
            pltpu.VMEM((GROUPS, cell_grp, R, LANES), jnp.float32),
            pltpu.SemaphoreType.DMA,
            pltpu.SemaphoreType.DMA((2,)),
            pltpu.SemaphoreType.DMA((GROUPS,)),
            pltpu.SemaphoreType.DMA((GROUPS,)),
            pltpu.SemaphoreType.DMA((GROUPS,)),
            pltpu.SemaphoreType.DMA((GROUPS,)),
        ],
        compiler_params=pltpu.CompilerParams(
            collective_id=0, has_side_effects=True, vmem_limit_bytes=48 * 1024 * 1024
        ),
    )(
        up_cells[0],
        piece_up[0],
        piece_owner.reshape(1, slots),
        piece_cell.reshape(1, slots),
        right_side.reshape(cells, U, R).swapaxes(1, 2),
        piece_rhs.reshape(slots, U, R).swapaxes(1, 2),
        up_blocks.reshape(2 * cells, U, U),
        inverses.reshape(cells, U, U),
        piece_blocks.reshape(slots, U, U),
    )
    return states.swapaxes(1, 2).reshape(1, cells, U * R)


def solution(mesh):
    sections, span = mesh.shape["stream"], mesh.shape["span"]
    span_x = 4 if span == 32 else 2
    sizes = (sections, span_x, span // span_x, 56, 48)
    in_specs = (
        P("stream", "span", None),
        P("stream", "span", None),
        P("stream", "span", None),
        P("stream", "span", None),
        P("stream", "span", None),
        P("stream", "span", None),
        P("stream", "span"),
        P("stream", "span", None),
        P("stream", "span"),
    )
    out_specs = P("stream", "span", None)
    return jax.shard_map(
        functools.partial(on_device, sizes),
        mesh=mesh,
        in_specs=in_specs,
        out_specs=out_specs,
        check_vma=False,
    )
```

```python
import functools

import jax
import jax.numpy as jnp
from jax import lax
from jax.experimental import pallas as pl
from jax.experimental.pallas import tpu as pltpu
from jax.sharding import PartitionSpec as P

U = 100
R = 16
LANES = 128
GROUPS = 2
CAP = 2
MSG = CAP * R
BLOCK = 4
HALF = 14
UP_LANE = 64
MESH = pl.DeviceIdType.MESH


def times_transposed(states, block):
    return lax.dot_general(
        states, block, (((1,), (1,)), ((), ())), preferred_element_type=jnp.float32
    )


def section_kernel(
    sizes,
    up_cells,
    owner_row,
    cell_row,
    up_row,
    right_side,
    piece_rhs,
    up_blocks,
    inverses,
    piece_blocks,
    out,
    face_t,
    inverse_t,
    piece_pad,
    rhs_pad,
    piece_rhs_pad,
    next_piece,
    next_rhs,
    coupling,
    table,
    next_table,
    own_slots,
    slots_next,
    index_out,
    index_in,
    selector,
    first_box,
    outbox,
    inbox,
    arrived_0,
    arrived_1,
    sent,
    owned,
    merged,
    table_sems,
    ship_sems,
    ship_recv_sems,
    index_sems,
    first_sems,
    outbox_sems,
    inbox_sems,
    sent_sems,
    arrived_sems,
):
    sections, span_x, span_y, cells, slots = sizes
    span = span_x * span_y
    cell_grp, slot_grp = cells // GROUPS, slots // GROUPS
    section = lax.axis_index("stream")
    me = lax.axis_index("span")
    me_x, me_y = me // span_y, me % span_y
    after, ahead = (section + 1) % sections, (section + sections - 1) % sections
    arrived = (arrived_0, arrived_1)
    remote = pl.ds(1, span - 1)
    is_first, is_last = section == 0, section == sections - 1

    def peer(turn):
        x = (me_x + turn // span_y) % span_x
        y = (me_y + turn % span_y) % span_y
        return x * span_y + y

    def whole_wait(ref, sem):
        pltpu.make_async_copy(ref, ref, sem).wait()

    barrier = pltpu.get_barrier_semaphore()

    @pl.loop(0, span)
    def _(turn):
        pl.semaphore_signal(
            barrier,
            inc=1,
            device_id={"stream": ahead, "span": peer(turn)},
            device_id_type=MESH,
        )

    @pl.loop(1, span)
    def _(turn):
        pl.semaphore_signal(barrier, inc=1, device_id={"span": peer(turn)}, device_id_type=MESH)

    pl.semaphore_signal(barrier, inc=1, device_id={"stream": after}, device_id_type=MESH)

    turn_col = lax.broadcasted_iota(jnp.int32, (span, slots), 0)
    slot_lane = lax.broadcasted_iota(jnp.int32, (span, slots), 1)
    match = owner_row[...] == peer(turn_col)
    lane = lax.broadcasted_iota(jnp.int32, (span, LANES), 1)
    mine = lane // MSG == lax.broadcasted_iota(jnp.int32, (span, LANES), 0) % BLOCK
    slot_values = jnp.zeros((span, LANES), jnp.int32)
    for group in range(GROUPS):
        indices = jnp.zeros((span, LANES), jnp.int32)
        named = match & (slot_lane // slot_grp == group)
        lowest = jnp.min(jnp.where(named, slot_lane, slots), axis=1, keepdims=True)
        highest = jnp.max(jnp.where(named, slot_lane, -1), axis=1, keepdims=True)
        found = (highest >= lowest, highest > lowest)
        for place, piece in enumerate((lowest, highest)):
            chosen = (slot_lane == piece) & found[place]
            piece = jnp.where(found[place], piece, group * slot_grp)
            target = jnp.sum(jnp.where(chosen, cell_row[...] + 1, 0), axis=1, keepdims=True)
            source = jnp.sum(jnp.where(chosen, up_row[...], 0), axis=1, keepdims=True)
            column = group * CAP + place
            slot_values = jnp.where(lane == column, piece, slot_values)
            slot_values = jnp.where(lane == GROUPS * CAP + column, source, slot_values)
            indices = jnp.where(mine & (lane // R % CAP == place), target, indices)
        index_out[:, group, :] = indices
    table[...] = slot_values
    table[:, UP_LANE : UP_LANE + slots] = jnp.broadcast_to(up_row[...], (span, slots))

    @pl.when(is_first)
    def _():
        pltpu.make_async_copy(table, own_slots, table_sems.at[0]).start()

    def padded(source, target, count):
        target[...] = jnp.zeros_like(target)

        @pl.loop(0, count)
        def _(i):
            target[i, : source.shape[1], : source.shape[2]] = source[i]

    def transposed(target, count):
        @pl.loop(0, count // BLOCK)
        def _(index):
            for j in range(BLOCK):
                i = index * BLOCK + j
                target[i] = target[i].astype(jnp.float32).T.astype(jnp.bfloat16)

    padded(piece_rhs, piece_rhs_pad, slots)
    padded(piece_blocks, piece_pad, slots)
    padded(right_side, rhs_pad, cells)

    pl.semaphore_wait(barrier, 2 * span)

    def shipments():
        return [
            pltpu.make_async_remote_copy(
                src_ref=source,
                dst_ref=target,
                send_sem=ship_sems.at[i],
                recv_sem=ship_recv_sems.at[i],
                device_id={"stream": ahead},
                device_id_type=MESH,
            )
            for i, (source, target) in enumerate(
                ((table, next_table), (piece_rhs_pad, next_rhs), (piece_pad, next_piece))
            )
        ]

    @pl.when(section > 0)
    def _():
        for copy in shipments():
            copy.start()

    index_in[0] = index_out[0]

    @pl.loop(1, span)
    def _(turn):
        pltpu.make_async_remote_copy(
            src_ref=index_out.at[turn],
            dst_ref=index_in.at[turn],
            send_sem=index_sems.at[0],
            recv_sem=index_sems.at[1],
            device_id={"span": peer(turn)},
            device_id_type=MESH,
        ).start()

    @pl.when(is_first)
    def _():
        pltpu.make_async_copy(table, own_slots, table_sems.at[0]).wait()
        for group in range(GROUPS):
            for place in range(CAP):
                piece = own_slots[0, group * CAP + place]
                inbox[group, 0, pl.ds(place * R, R), :] = piece_rhs_pad[piece]

            @pl.loop(1, span)
            def _(turn):
                for place in range(CAP):
                    piece = own_slots[turn, group * CAP + place]
                    first_box[group, turn, pl.ds(place * R, R), :] = piece_rhs_pad[piece]
                pltpu.make_async_remote_copy(
                    src_ref=first_box.at[group, turn],
                    dst_ref=inbox.at[group, turn],
                    send_sem=first_sems.at[group],
                    recv_sem=inbox_sems.at[group],
                    device_id={"span": peer(turn)},
                    device_id_type=MESH,
                ).start()

    padded(inverses, inverse_t, cells)
    transposed(inverse_t, cells)

    @pl.when(jnp.logical_not(is_last))
    def _():
        whole_wait(next_table, ship_recv_sems.at[0])
        to_slots = pltpu.make_async_copy(next_table, slots_next, table_sems.at[1])
        to_slots.start()
        whole_wait(next_rhs, ship_recv_sems.at[1])
        whole_wait(next_piece, ship_recv_sems.at[2])
        to_slots.wait()
        for group in range(GROUPS):

            @pl.loop(0, slot_grp // BLOCK)
            def _(index):
                for j in range(BLOCK):
                    piece = group * slot_grp + index * BLOCK + j
                    cell = group * cell_grp + slots_next[0, UP_LANE + piece]
                    coupling[piece] = times_transposed(inverse_t[cell], next_piece[piece]).astype(
                        jnp.bfloat16
                    )

    @pl.when(section > 0)
    def _():
        padded(up_blocks, face_t, 2 * cells)
        transposed(face_t, 2 * cells)

    whole_wait(index_in.at[remote], index_sems.at[1])
    row = lax.broadcasted_iota(jnp.int32, (cell_grp * R, LANES), 0)
    column = lax.broadcasted_iota(jnp.int32, (cell_grp * R, LANES), 1)
    same_side = row % R == column % R
    for group in range(GROUPS):
        for part in range(span // BLOCK):
            named = index_in[BLOCK * part, pl.ds(group, 1), :]
            for j in range(1, BLOCK):
                named = named + index_in[BLOCK * part + j, pl.ds(group, 1), :]
            hit = same_side & (row // R + 1 == named)
            selector[group, :, pl.ds(part * LANES, LANES)] = hit.astype(jnp.bfloat16)

    def downstream(group, half):
        cells_of = pl.ds(half * HALF, HALF)
        return pltpu.make_async_remote_copy(
            src_ref=sent.at[group, cells_of],
            dst_ref=arrived[group].at[cells_of],
            send_sem=sent_sems.at[group],
            recv_sem=arrived_sems.at[group],
            device_id={"stream": after},
            device_id_type=MESH,
        )

    def own_terms(group):
        @pl.when(is_first)
        def _():
            owned[group] = rhs_pad[pl.ds(group * cell_grp, cell_grp)].astype(jnp.float32)

        @pl.when(section > 0)
        def _():
            whole_wait(arrived[group], arrived_sems.at[group])

            @pl.loop(0, cell_grp // 7)
            def _(index):
                for j in range(7):
                    cell = index * 7 + j
                    whole = group * cell_grp + cell
                    total = rhs_pad[whole].astype(jnp.float32)
                    for face in range(2):
                        near = arrived[group][up_cells[whole, face]]
                        total = total - jnp.dot(
                            near, face_t[2 * whole + face], preferred_element_type=jnp.float32
                        )
                    owned[group, cell] = total

    def merge(group):
        @pl.when(is_first)
        def _():
            whole_wait(inbox.at[group, remote], inbox_sems.at[group])

        @pl.when(section > 0)
        def _():
            whole_wait(inbox.at[group], inbox_sems.at[group])

        messages = inbox[group].reshape(span * MSG, LANES)
        summed = jnp.dot(selector[group], messages, preferred_element_type=jnp.float32)
        total = owned[group] + summed.reshape(cell_grp, R, LANES)
        merged[group] = total.astype(jnp.bfloat16)

    def send_partials(group):
        order_x = sorted(range(span_x), key=lambda x: -min(x, span_x - x))

        @pl.loop(0, span_y // 2)
        def _(index):
            turns = []
            for y in (span_y // 2 + index, span_y // 2 - 1 - index):
                for x in order_x:
                    turns.append(x * span_y + y)
            for turn in turns:
                for place in range(CAP):
                    column = group * CAP + place
                    piece = slots_next[turn, column]
                    near = merged[group, slots_next[turn, GROUPS * CAP + column]]
                    term = next_rhs[piece].astype(jnp.float32) - jnp.dot(
                        near, coupling[piece], preferred_element_type=jnp.float32
                    )
                    outbox[group, turn, pl.ds(place * R, R), :] = term.astype(jnp.bfloat16)
                pltpu.make_async_remote_copy(
                    src_ref=outbox.at[group, turn],
                    dst_ref=inbox.at[group, turn],
                    send_sem=outbox_sems.at[group],
                    recv_sem=inbox_sems.at[group],
                    device_id={"stream": after, "span": peer(turn)},
                    device_id_type=MESH,
                ).start()

    def solve(group):
        for half in range(cell_grp // HALF):
            for j in range(HALF):
                cell = half * HALF + j
                sent[group, cell] = jnp.dot(
                    merged[group, cell],
                    inverse_t[group * cell_grp + cell],
                    preferred_element_type=jnp.float32,
                ).astype(jnp.bfloat16)

            @pl.when(jnp.logical_not(is_last))
            def _():
                downstream(group, half).start()

    for group in range(GROUPS):
        own_terms(group)
        merge(group)

        @pl.when(jnp.logical_not(is_last))
        def _():
            send_partials(group)

        solve(group)

    for group in range(GROUPS):
        out[pl.ds(group * cell_grp, cell_grp)] = sent[group, :, :, :U]

    whole_wait(index_out.at[remote], index_sems.at[0])

    @pl.when(section > 0)
    def _():
        for copy in shipments():
            copy.wait_send()

    @pl.when(is_first)
    def _():
        for group in range(GROUPS):
            whole_wait(first_box.at[group, remote], first_sems.at[group])

    @pl.when(jnp.logical_not(is_last))
    def _():
        for group in range(GROUPS):
            whole_wait(outbox.at[group], outbox_sems.at[group])
            whole_wait(sent.at[group], sent_sems.at[group])


def on_device(
    sizes,
    right_side,
    up_blocks,
    inverses,
    up_cells,
    piece_rhs,
    piece_blocks,
    piece_up,
    piece_owner,
    piece_cell,
):
    sections, span_x, span_y, cells, slots = sizes
    span = span_x * span_y
    cell_grp = cells // GROUPS
    vmem = pl.BlockSpec(memory_space=pltpu.VMEM)
    smem = pl.BlockSpec(memory_space=pltpu.SMEM)
    bf16 = jnp.bfloat16
    states = pl.pallas_call(
        functools.partial(section_kernel, sizes),
        out_shape=jax.ShapeDtypeStruct((cells, R, U), bf16),
        in_specs=[smem] + [vmem] * 8,
        out_specs=vmem,
        scratch_shapes=[
            pltpu.VMEM((2 * cells, LANES, LANES), bf16),
            pltpu.VMEM((cells, LANES, LANES), bf16),
            pltpu.VMEM((slots, LANES, LANES), bf16),
            pltpu.VMEM((cells, R, LANES), bf16),
            pltpu.VMEM((slots, R, LANES), bf16),
            pltpu.VMEM((slots, LANES, LANES), bf16),
            pltpu.VMEM((slots, R, LANES), bf16),
            pltpu.VMEM((slots, LANES, LANES), bf16),
            pltpu.VMEM((span, LANES), jnp.int32),
            pltpu.VMEM((span, LANES), jnp.int32),
            pltpu.SMEM((span, LANES), jnp.int32),
            pltpu.SMEM((span, LANES), jnp.int32),
            pltpu.VMEM((span, GROUPS, LANES), jnp.int32),
            pltpu.VMEM((span, GROUPS, LANES), jnp.int32),
            pltpu.VMEM((GROUPS, cell_grp * R, span * MSG), bf16),
            pltpu.VMEM((GROUPS, span, MSG, LANES), bf16),
            pltpu.VMEM((GROUPS, span, MSG, LANES), bf16),
            pltpu.VMEM((GROUPS, span, MSG, LANES), bf16),
            pltpu.VMEM((cell_grp, R, LANES), bf16),
            pltpu.VMEM((cell_grp, R, LANES), bf16),
            pltpu.VMEM((GROUPS, cell_grp, R, LANES), bf16),
            pltpu.VMEM((GROUPS, cell_grp, R, LANES), jnp.float32),
            pltpu.VMEM((GROUPS, cell_grp, R, LANES), bf16),
            pltpu.SemaphoreType.DMA((2,)),
            pltpu.SemaphoreType.DMA((3,)),
            pltpu.SemaphoreType.DMA((3,)),
            pltpu.SemaphoreType.DMA((2,)),
            pltpu.SemaphoreType.DMA((GROUPS,)),
            pltpu.SemaphoreType.DMA((GROUPS,)),
            pltpu.SemaphoreType.DMA((GROUPS,)),
            pltpu.SemaphoreType.DMA((GROUPS,)),
            pltpu.SemaphoreType.DMA((GROUPS,)),
        ],
        compiler_params=pltpu.CompilerParams(
            collective_id=0, has_side_effects=True, vmem_limit_bytes=48 * 1024 * 1024
        ),
    )(
        up_cells[0],
        piece_owner.reshape(1, slots),
        piece_cell.reshape(1, slots),
        piece_up.reshape(1, slots),
        right_side.reshape(cells, U, R).swapaxes(1, 2),
        piece_rhs.reshape(slots, U, R).swapaxes(1, 2),
        up_blocks.reshape(2 * cells, U, U),
        inverses.reshape(cells, U, U),
        piece_blocks.reshape(slots, U, U),
    )
    return states.swapaxes(1, 2).reshape(1, cells, U * R)


def solution(mesh):
    sections, span = mesh.shape["stream"], mesh.shape["span"]
    span_x = 4 if span == 32 else 2
    sizes = (sections, span_x, span // span_x, 56, 48)
    in_specs = (
        P("stream", "span", None),
        P("stream", "span", None),
        P("stream", "span", None),
        P("stream", "span", None),
        P("stream", "span", None),
        P("stream", "span", None),
        P("stream", "span"),
        P("stream", "span", None),
        P("stream", "span"),
    )
    out_specs = P("stream", "span", None)
    return jax.shard_map(
        functools.partial(on_device, sizes),
        mesh=mesh,
        in_specs=in_specs,
        out_specs=out_specs,
        check_vma=False,
    )
```

```python
import functools

import jax
import jax.numpy as jnp
from jax import lax
from jax.experimental import pallas as pl
from jax.experimental.pallas import tpu as pltpu
from jax.sharding import PartitionSpec as P

U = 100
R = 16
LANES = 128
GROUPS = 2
CAP = 2
MSG = CAP * R
BLOCK = 4
HALF = 14
UP_LANE = 64
STRIDE = 136
FIRST_ROWS = 32
MESH = pl.DeviceIdType.MESH


def times_transposed(states, block):
    return lax.dot_general(
        states, block, (((1,), (1,)), ((), ())), preferred_element_type=jnp.float32
    )


def section_kernel(
    sizes,
    up_cells,
    owner_row,
    cell_row,
    up_row,
    right_side,
    piece_rhs,
    up_blocks,
    inverses,
    piece_blocks,
    out,
    face_flat,
    inverse_flat,
    piece_flat,
    spread,
    face_t,
    inverse_t,
    rhs_pad,
    piece_rhs_pad,
    next_rhs,
    coupling,
    table,
    next_table,
    own_slots,
    slots_next,
    index_out,
    index_in,
    selector,
    first_box,
    outbox,
    inbox,
    arrived_0,
    arrived_1,
    sent,
    owned,
    merged,
    load_sems,
    table_sems,
    ship_sems,
    ship_recv_sems,
    index_sems,
    first_sems,
    outbox_sems,
    inbox_sems,
    sent_sems,
    arrived_sems,
):
    sections, span_x, span_y, cells, slots = sizes
    span = span_x * span_y
    cell_grp, slot_grp = cells // GROUPS, slots // GROUPS
    section = lax.axis_index("stream")
    me = lax.axis_index("span")
    me_x, me_y = me // span_y, me % span_y
    after, ahead = (section + 1) % sections, (section + sections - 1) % sections
    arrived = (arrived_0, arrived_1)
    near = span // 2
    others = pl.ds(0, span - 1)
    is_first, is_last = section == 0, section == sections - 1

    order_x = sorted(range(span_x), key=lambda x: -min(x, span_x - x))

    def peer(turn):
        pair, place = turn // (2 * span_x), turn % span_x
        upper = turn // span_x % 2 == 0
        y = jnp.where(upper, span_y // 2 + pair, span_y // 2 - 1 - pair)
        x = sum(order_x[i] * jnp.where(place == i, 1, 0) for i in range(span_x))
        return (me_x + x) % span_x * span_y + (me_y + y) % span_y

    def whole_wait(ref, sem):
        pltpu.make_async_copy(ref, ref, sem).wait()

    loads = [
        pltpu.make_async_copy(inverses, inverse_flat, load_sems.at[0]),
        pltpu.make_async_copy(up_blocks, face_flat, load_sems.at[1]),
    ]
    for load in loads:
        load.start()

    barrier = pltpu.get_barrier_semaphore()

    @pl.loop(0, span)
    def _(turn):
        pl.semaphore_signal(
            barrier,
            inc=1,
            device_id={"stream": ahead, "span": peer(turn)},
            device_id_type=MESH,
        )

    @pl.loop(0, span - 1)
    def _(turn):
        pl.semaphore_signal(barrier, inc=1, device_id={"span": peer(turn)}, device_id_type=MESH)

    pl.semaphore_signal(barrier, inc=1, device_id={"stream": after}, device_id_type=MESH)

    turn_col = lax.broadcasted_iota(jnp.int32, (span, slots), 0)
    slot_lane = lax.broadcasted_iota(jnp.int32, (span, slots), 1)
    match = owner_row[...] == peer(turn_col)
    lane = lax.broadcasted_iota(jnp.int32, (span, LANES), 1)
    mine = lane // MSG == lax.broadcasted_iota(jnp.int32, (span, LANES), 0) % BLOCK
    slot_values = jnp.zeros((span, LANES), jnp.int32)
    for group in range(GROUPS):
        indices = jnp.zeros((span, LANES), jnp.int32)
        named = match & (slot_lane // slot_grp == group)
        lowest = jnp.min(jnp.where(named, slot_lane, slots), axis=1, keepdims=True)
        highest = jnp.max(jnp.where(named, slot_lane, -1), axis=1, keepdims=True)
        found = (highest >= lowest, highest > lowest)
        for place, piece in enumerate((lowest, highest)):
            chosen = (slot_lane == piece) & found[place]
            piece = jnp.where(found[place], piece, group * slot_grp)
            target = jnp.sum(jnp.where(chosen, cell_row[...] + 1, 0), axis=1, keepdims=True)
            source = jnp.sum(jnp.where(chosen, up_row[...], 0), axis=1, keepdims=True)
            column = group * CAP + place
            slot_values = jnp.where(lane == column, piece, slot_values)
            slot_values = jnp.where(lane == GROUPS * CAP + column, source, slot_values)
            indices = jnp.where(mine & (lane // R % CAP == place), target, indices)
        index_out[:, group, :] = indices
    table[...] = slot_values
    table[:, UP_LANE : UP_LANE + slots] = jnp.broadcast_to(up_row[...], (span, slots))

    @pl.when(is_first)
    def _():
        pltpu.make_async_copy(table, own_slots, table_sems.at[0]).start()

    def padded(source, target, count):
        target[...] = jnp.zeros_like(target)

        @pl.loop(0, count)
        def _(i):
            target[i, : source.shape[1], : source.shape[2]] = source[i]

    def unfolded(flat, offset, base, count):
        def tile(block, height):
            for i in range(U):
                start = offset + U * i
                rows = flat[pl.ds(block, height), start : start + U]
                spread[pl.ds(block * STRIDE + i, height, stride=STRIDE), :U] = rows.astype(
                    jnp.float32
                )

        @pl.loop(0, count // 16)
        def _(index):
            tile(pl.multiple_of(base + index * 16, 16), 16)

        if count % 16:
            tile(base + count // 16 * 16, count % 16)

    def matrix(block):
        return spread[pl.ds(block * STRIDE, LANES), :]

    def transposed(target, base, count):
        @pl.loop(0, count // BLOCK)
        def _(index):
            for j in range(BLOCK):
                block = index * BLOCK + j
                target[base + block] = matrix(block).T.astype(jnp.bfloat16)

    spread[...] = jnp.zeros_like(spread)
    padded(piece_rhs, piece_rhs_pad, slots)
    padded(right_side, rhs_pad, cells)

    pl.semaphore_wait(barrier, 2 * span)

    def shipments():
        parts = (pl.ds(0, FIRST_ROWS), pl.ds(FIRST_ROWS, slots - FIRST_ROWS))
        return [
            pltpu.make_async_remote_copy(
                src_ref=source,
                dst_ref=target,
                send_sem=ship_sems.at[i],
                recv_sem=ship_recv_sems.at[i],
                device_id={"stream": ahead},
                device_id_type=MESH,
            )
            for i, (source, target) in enumerate(
                (
                    (table, next_table),
                    (piece_blocks.at[parts[0]], piece_flat.at[parts[0]]),
                    (piece_rhs_pad, next_rhs),
                    (piece_blocks.at[parts[1]], piece_flat.at[parts[1]]),
                )
            )
        ]

    @pl.when(section > 0)
    def _():
        for copy in shipments():
            copy.start()

    index_in[span - 1] = index_out[span - 1]

    @pl.loop(0, span - 1)
    def _(turn):
        pltpu.make_async_remote_copy(
            src_ref=index_out.at[turn],
            dst_ref=index_in.at[turn],
            send_sem=index_sems.at[0],
            recv_sem=index_sems.at[1],
            device_id={"span": peer(turn)},
            device_id_type=MESH,
        ).start()

    @pl.when(is_first)
    def _():
        pltpu.make_async_copy(table, own_slots, table_sems.at[0]).wait()
        for group in range(GROUPS):
            for place in range(CAP):
                piece = own_slots[span - 1, group * CAP + place]
                inbox[group, span - 1, pl.ds(place * R, R), :] = piece_rhs_pad[piece]

            @pl.loop(0, span - 1)
            def _(turn):
                for place in range(CAP):
                    piece = own_slots[turn, group * CAP + place]
                    first_box[group, turn, pl.ds(place * R, R), :] = piece_rhs_pad[piece]
                pltpu.make_async_remote_copy(
                    src_ref=first_box.at[group, turn],
                    dst_ref=inbox.at[group, turn],
                    send_sem=first_sems.at[group],
                    recv_sem=inbox_sems.at[group, turn // near],
                    device_id={"span": peer(turn)},
                    device_id_type=MESH,
                ).start()

    loads[0].wait()
    unfolded(inverse_flat, 0, 0, cells)
    transposed(inverse_t, 0, cells)

    @pl.when(jnp.logical_not(is_last))
    def _():
        whole_wait(next_table, ship_recv_sems.at[0])
        to_slots = pltpu.make_async_copy(next_table, slots_next, table_sems.at[1])
        to_slots.start()
        to_slots.wait()
        for group in range(GROUPS):
            base = group * slot_grp
            if group == 0:
                whole_wait(piece_flat.at[pl.ds(0, FIRST_ROWS)], ship_recv_sems.at[1])
                unfolded(piece_flat, 0, 0, FIRST_ROWS)
            else:
                whole_wait(
                    piece_flat.at[pl.ds(FIRST_ROWS, slots - FIRST_ROWS)], ship_recv_sems.at[3]
                )
                unfolded(piece_flat, 0, FIRST_ROWS, slots - FIRST_ROWS)

            @pl.loop(0, slot_grp // 8)
            def _(index):
                for j in range(8):
                    block = index * 8 + j
                    cell = group * cell_grp + slots_next[0, UP_LANE + base + block]
                    coupling[base + block] = times_transposed(
                        inverse_t[cell], matrix(base + block).astype(jnp.bfloat16)
                    ).astype(jnp.bfloat16)

        whole_wait(next_rhs, ship_recv_sems.at[2])

    loads[1].wait()

    @pl.when(section > 0)
    def _():
        for face in range(2):
            unfolded(face_flat, face * U * U, 0, cells)
            transposed(face_t, face * cells, cells)

    whole_wait(index_in.at[others], index_sems.at[1])
    row = lax.broadcasted_iota(jnp.int32, (cell_grp * R, LANES), 0)
    column = lax.broadcasted_iota(jnp.int32, (cell_grp * R, LANES), 1)
    same_side = row % R == column % R
    for group in range(GROUPS):
        for part in range(span // BLOCK):
            named = index_in[BLOCK * part, pl.ds(group, 1), :]
            for j in range(1, BLOCK):
                named = named + index_in[BLOCK * part + j, pl.ds(group, 1), :]
            hit = same_side & (row // R + 1 == named)
            half, place = divmod(part * BLOCK, near)
            selector[group, half, :, pl.ds(place * MSG, LANES)] = hit.astype(jnp.bfloat16)

    def downstream(group, half):
        cells_of = pl.ds(half * HALF, HALF)
        return pltpu.make_async_remote_copy(
            src_ref=sent.at[group, cells_of],
            dst_ref=arrived[group].at[cells_of],
            send_sem=sent_sems.at[group],
            recv_sem=arrived_sems.at[group],
            device_id={"stream": after},
            device_id_type=MESH,
        )

    def own_terms(group):
        @pl.when(is_first)
        def _():
            owned[group] = rhs_pad[pl.ds(group * cell_grp, cell_grp)].astype(jnp.float32)

        @pl.when(section > 0)
        def _():
            whole_wait(arrived[group], arrived_sems.at[group])

            @pl.loop(0, cell_grp // 7)
            def _(index):
                for j in range(7):
                    cell = index * 7 + j
                    whole = group * cell_grp + cell
                    total = rhs_pad[whole].astype(jnp.float32)
                    for face in range(2):
                        state = arrived[group][up_cells[face, whole]]
                        total = total - jnp.dot(
                            state, face_t[face * cells + whole], preferred_element_type=jnp.float32
                        )
                    owned[group, cell] = total

    def merge(group):
        total = owned[group]
        for half, part in ((1, pl.ds(near, near)), (0, pl.ds(0, near))):

            @pl.when(is_first)
            def _():
                known = pl.ds(near, near - 1) if half else part
                whole_wait(inbox.at[group, known], inbox_sems.at[group, half])

            @pl.when(section > 0)
            def _():
                whole_wait(inbox.at[group, part], inbox_sems.at[group, half])

            messages = inbox[group, part].reshape(near * MSG, LANES)
            summed = jnp.dot(
                selector[group, half], messages, preferred_element_type=jnp.float32
            ).reshape(cell_grp, R, LANES)
            if half:
                owned[group] = total + summed
            else:
                merged[group] = (owned[group] + summed).astype(jnp.bfloat16)

    def send_partials(group):
        @pl.loop(0, span // 8)
        def _(index):
            for j in range(8):
                turn = index * 8 + j
                for place in range(CAP):
                    column = group * CAP + place
                    piece = slots_next[turn, column]
                    state = merged[group, slots_next[turn, GROUPS * CAP + column]]
                    term = next_rhs[piece].astype(jnp.float32) - jnp.dot(
                        state, coupling[piece], preferred_element_type=jnp.float32
                    )
                    outbox[group, turn, pl.ds(place * R, R), :] = term.astype(jnp.bfloat16)
                pltpu.make_async_remote_copy(
                    src_ref=outbox.at[group, turn],
                    dst_ref=inbox.at[group, turn],
                    send_sem=outbox_sems.at[group],
                    recv_sem=inbox_sems.at[group, turn // near],
                    device_id={"stream": after, "span": peer(turn)},
                    device_id_type=MESH,
                ).start()

    def solve(group):
        for half in range(cell_grp // HALF):
            for j in range(HALF):
                cell = half * HALF + j
                sent[group, cell] = jnp.dot(
                    merged[group, cell],
                    inverse_t[group * cell_grp + cell],
                    preferred_element_type=jnp.float32,
                ).astype(jnp.bfloat16)

            @pl.when(jnp.logical_not(is_last))
            def _():
                downstream(group, half).start()

    for group in range(GROUPS):
        own_terms(group)
        merge(group)

        @pl.when(jnp.logical_not(is_last))
        def _():
            send_partials(group)

        solve(group)

    for group in range(GROUPS):
        out[pl.ds(group * cell_grp, cell_grp)] = sent[group, :, :, :U]

    whole_wait(index_out.at[others], index_sems.at[0])

    @pl.when(section > 0)
    def _():
        for copy in shipments():
            copy.wait_send()

    @pl.when(is_first)
    def _():
        for group in range(GROUPS):
            whole_wait(first_box.at[group, others], first_sems.at[group])

    @pl.when(jnp.logical_not(is_last))
    def _():
        for group in range(GROUPS):
            whole_wait(outbox.at[group], outbox_sems.at[group])
            whole_wait(sent.at[group], sent_sems.at[group])


def on_device(
    sizes,
    right_side,
    up_blocks,
    inverses,
    up_cells,
    piece_rhs,
    piece_blocks,
    piece_up,
    piece_owner,
    piece_cell,
):
    sections, span_x, span_y, cells, slots = sizes
    span = span_x * span_y
    cell_grp = cells // GROUPS
    vmem = pl.BlockSpec(memory_space=pltpu.VMEM)
    smem = pl.BlockSpec(memory_space=pltpu.SMEM)
    bf16 = jnp.bfloat16
    states = pl.pallas_call(
        functools.partial(section_kernel, sizes),
        out_shape=jax.ShapeDtypeStruct((cells, R, U), bf16),
        in_specs=[smem] + [vmem] * 5 + [pl.BlockSpec(memory_space=pl.ANY)] * 3,
        out_specs=vmem,
        scratch_shapes=[
            pltpu.VMEM((cells, 2 * U * U), bf16),
            pltpu.VMEM((cells, U * U), bf16),
            pltpu.VMEM((slots, U * U), bf16),
            pltpu.VMEM((cells * STRIDE, LANES), jnp.float32),
            pltpu.VMEM((2 * cells, LANES, LANES), bf16),
            pltpu.VMEM((cells, LANES, LANES), bf16),
            pltpu.VMEM((cells, R, LANES), bf16),
            pltpu.VMEM((slots, R, LANES), bf16),
            pltpu.VMEM((slots, R, LANES), bf16),
            pltpu.VMEM((slots, LANES, LANES), bf16),
            pltpu.VMEM((span, LANES), jnp.int32),
            pltpu.VMEM((span, LANES), jnp.int32),
            pltpu.SMEM((span, LANES), jnp.int32),
            pltpu.SMEM((span, LANES), jnp.int32),
            pltpu.VMEM((span, GROUPS, LANES), jnp.int32),
            pltpu.VMEM((span, GROUPS, LANES), jnp.int32),
            pltpu.VMEM((GROUPS, 2, cell_grp * R, span // 2 * MSG), bf16),
            pltpu.VMEM((GROUPS, span, MSG, LANES), bf16),
            pltpu.VMEM((GROUPS, span, MSG, LANES), bf16),
            pltpu.VMEM((GROUPS, span, MSG, LANES), bf16),
            pltpu.VMEM((cell_grp, R, LANES), bf16),
            pltpu.VMEM((cell_grp, R, LANES), bf16),
            pltpu.VMEM((GROUPS, cell_grp, R, LANES), bf16),
            pltpu.VMEM((GROUPS, cell_grp, R, LANES), jnp.float32),
            pltpu.VMEM((GROUPS, cell_grp, R, LANES), bf16),
            pltpu.SemaphoreType.DMA((2,)),
            pltpu.SemaphoreType.DMA((2,)),
            pltpu.SemaphoreType.DMA((4,)),
            pltpu.SemaphoreType.DMA((4,)),
            pltpu.SemaphoreType.DMA((2,)),
            pltpu.SemaphoreType.DMA((GROUPS,)),
            pltpu.SemaphoreType.DMA((GROUPS,)),
            pltpu.SemaphoreType.DMA((GROUPS, 2)),
            pltpu.SemaphoreType.DMA((GROUPS,)),
            pltpu.SemaphoreType.DMA((GROUPS,)),
        ],
        compiler_params=pltpu.CompilerParams(
            collective_id=0, has_side_effects=True, vmem_limit_bytes=48 * 1024 * 1024
        ),
    )(
        up_cells[0].T,
        piece_owner.reshape(1, slots),
        piece_cell.reshape(1, slots),
        piece_up.reshape(1, slots),
        right_side.reshape(cells, U, R).swapaxes(1, 2),
        piece_rhs.reshape(slots, U, R).swapaxes(1, 2),
        up_blocks.reshape(cells, 2 * U * U),
        inverses.reshape(cells, U * U),
        piece_blocks.reshape(slots, U * U),
    )
    return states.swapaxes(1, 2).reshape(1, cells, U * R)


def solution(mesh):
    sections, span = mesh.shape["stream"], mesh.shape["span"]
    span_x = 4 if span == 32 else 2
    sizes = (sections, span_x, span // span_x, 56, 48)
    in_specs = (
        P("stream", "span", None),
        P("stream", "span", None),
        P("stream", "span", None),
        P("stream", "span", None),
        P("stream", "span", None),
        P("stream", "span", None),
        P("stream", "span"),
        P("stream", "span", None),
        P("stream", "span"),
    )
    out_specs = P("stream", "span", None)
    return jax.shard_map(
        functools.partial(on_device, sizes),
        mesh=mesh,
        in_specs=in_specs,
        out_specs=out_specs,
        check_vma=False,
    )
```

```python
import functools

import jax
import jax.numpy as jnp
from jax import lax
from jax.experimental import pallas as pl
from jax.experimental.pallas import tpu as pltpu
from jax.sharding import PartitionSpec as P

U = 100
R = 16
LANES = 128
GROUPS = 2
CAP = 2
MSG = CAP * R
BLOCK = 4
HALF = 14
UP_LANE = 64
STRIDE = 136
FIRST_ROWS = 32
MESH = pl.DeviceIdType.MESH


def times_transposed(states, block):
    return lax.dot_general(
        states, block, (((1,), (1,)), ((), ())), preferred_element_type=jnp.float32
    )


def section_kernel(
    sizes,
    up_cells,
    owner_row,
    cell_row,
    up_row,
    right_side,
    piece_rhs,
    up_blocks,
    inverses,
    piece_blocks,
    out,
    face_flat,
    inverse_flat,
    piece_flat,
    spread,
    face_t,
    inverse_t,
    rhs_pad,
    piece_rhs_pad,
    next_rhs_0,
    next_rhs_1,
    coupling,
    table,
    next_table,
    own_slots,
    slots_next,
    index_out,
    index_in,
    selector,
    first_box,
    outbox,
    inbox,
    arrived_0,
    arrived_1,
    sent,
    owned,
    merged,
    load_sems,
    table_sems,
    ship_sems,
    ship_recv_sems,
    index_sems,
    first_sems,
    outbox_sems,
    inbox_sems,
    sent_sems,
    arrived_sems,
):
    sections, span_x, span_y, cells, slots = sizes
    span = span_x * span_y
    cell_grp, slot_grp = cells // GROUPS, slots // GROUPS
    section = lax.axis_index("stream")
    me = lax.axis_index("span")
    me_x, me_y = lax.div(me, span_y), lax.rem(me, span_y)
    after, ahead = lax.rem(section + 1, sections), lax.rem(section + sections - 1, sections)
    arrived = (arrived_0, arrived_1)
    next_rhs = (next_rhs_0, next_rhs_1)
    near = span // 2
    others = pl.ds(0, span - 1)
    is_first, is_last = section == 0, section == sections - 1

    order_x = sorted(range(span_x), key=lambda x: -min(x, span_x - x))

    def peer(turn):
        pair, place = turn // (2 * span_x), turn % span_x
        upper = turn // span_x % 2 == 0
        y = jnp.where(upper, span_y // 2 + pair, span_y // 2 - 1 - pair)
        x = sum(order_x[i] * jnp.where(place == i, 1, 0) for i in range(span_x))
        return (me_x + x) % span_x * span_y + (me_y + y) % span_y

    pairs, places = span_y // 2, 2 * span_x
    row_of = [lax.rem(me_x + x, span_x) * span_y for x in order_x]

    def peer_at(pair, place):
        y = span_y // 2 + pair if place < span_x else span_y // 2 - 1 - pair
        return row_of[place % span_x] + lax.rem(me_y + y, span_y)

    def for_others(act):
        @pl.loop(0, pairs)
        def _(pair):
            for place in range(places - 1):
                act(pair * places + place, peer_at(pair, place))

            @pl.when(pair < pairs - 1)
            def _():
                act(pair * places + places - 1, peer_at(pair, places - 1))

    def whole_wait(ref, sem):
        pltpu.make_async_copy(ref, ref, sem).wait()

    loads = [
        pltpu.make_async_copy(inverses, inverse_flat, load_sems.at[0]),
        pltpu.make_async_copy(up_blocks, face_flat, load_sems.at[1]),
    ]
    for load in loads:
        load.start()

    barrier = pltpu.get_barrier_semaphore()

    def greet(turn, device):
        pl.semaphore_signal(barrier, inc=1, device_id={"span": device}, device_id_type=MESH)

    @pl.loop(0, pairs)
    def _(pair):
        for place in range(places):
            pl.semaphore_signal(
                barrier,
                inc=1,
                device_id={"stream": ahead, "span": peer_at(pair, place)},
                device_id_type=MESH,
            )

    for_others(greet)
    pl.semaphore_signal(barrier, inc=1, device_id={"stream": after}, device_id_type=MESH)

    turn_col = lax.broadcasted_iota(jnp.int32, (span, slots), 0)
    slot_lane = lax.broadcasted_iota(jnp.int32, (span, slots), 1)
    match = owner_row[...] == peer(turn_col)
    lane = lax.broadcasted_iota(jnp.int32, (span, LANES), 1)
    mine = lane // MSG == lax.broadcasted_iota(jnp.int32, (span, LANES), 0) % BLOCK
    slot_values = jnp.zeros((span, LANES), jnp.int32)
    for group in range(GROUPS):
        indices = jnp.zeros((span, LANES), jnp.int32)
        named = match & (slot_lane // slot_grp == group)
        lowest = jnp.min(jnp.where(named, slot_lane, slots), axis=1, keepdims=True)
        highest = jnp.max(jnp.where(named, slot_lane, -1), axis=1, keepdims=True)
        found = (highest >= lowest, highest > lowest)
        for place, piece in enumerate((lowest, highest)):
            chosen = (slot_lane == piece) & found[place]
            piece = jnp.where(found[place], piece, group * slot_grp)
            target = jnp.sum(jnp.where(chosen, cell_row[...] + 1, 0), axis=1, keepdims=True)
            source = jnp.sum(jnp.where(chosen, up_row[...], 0), axis=1, keepdims=True)
            column = group * CAP + place
            slot_values = jnp.where(lane == column, piece, slot_values)
            slot_values = jnp.where(lane == GROUPS * CAP + column, source, slot_values)
            indices = jnp.where(mine & (lane // R % CAP == place), target, indices)
        index_out[:, group, :] = indices
    table[...] = slot_values
    table[:, UP_LANE : UP_LANE + slots] = jnp.broadcast_to(up_row[...], (span, slots))

    @pl.when(is_first)
    def _():
        pltpu.make_async_copy(table, own_slots, table_sems.at[0]).start()

    def padded(source, target, count):
        target[...] = jnp.zeros_like(target)

        @pl.loop(0, count)
        def _(i):
            target[i, : source.shape[1], : source.shape[2]] = source[i]

    def unfolded(flat, offset, base, count):
        def tile(block, height):
            for i in range(U):
                start = offset + U * i
                rows = flat[pl.ds(block, height), start : start + U]
                spread[pl.ds(block * STRIDE + i, height, stride=STRIDE), :U] = rows.astype(
                    jnp.float32
                )

        @pl.loop(0, count // 16)
        def _(index):
            tile(pl.multiple_of(base + index * 16, 16), 16)

        if count % 16:
            tile(base + count // 16 * 16, count % 16)

    def matrix(block):
        return spread[pl.ds(block * STRIDE, LANES), :]

    def transposed(target, base, count):
        @pl.loop(0, count // BLOCK)
        def _(index):
            for j in range(BLOCK):
                block = index * BLOCK + j
                target[base + block] = matrix(block).T.astype(jnp.bfloat16)

    spread[...] = jnp.zeros_like(spread)
    padded(piece_rhs, piece_rhs_pad, slots)
    padded(right_side, rhs_pad, cells)

    loads[0].wait()
    unfolded(inverse_flat, 0, 0, cells)
    transposed(inverse_t, 0, cells)

    loads[1].wait()

    @pl.when(section > 0)
    def _():
        for face in range(2):
            unfolded(face_flat, face * U * U, 0, cells)

            @pl.loop(0, cells // BLOCK)
            def _(index):
                for j in range(BLOCK):
                    cell = index * BLOCK + j
                    face_t[cell, pl.ds(face * LANES, LANES), :] = matrix(cell).T.astype(
                        jnp.bfloat16
                    )

    pl.semaphore_wait(barrier, 2 * span)

    halves = (pl.ds(0, slot_grp), pl.ds(slot_grp, slot_grp))
    parts = (pl.ds(0, FIRST_ROWS), pl.ds(FIRST_ROWS, slots - FIRST_ROWS))

    def shipments():
        return [
            pltpu.make_async_remote_copy(
                src_ref=source,
                dst_ref=target,
                send_sem=ship_sems.at[i],
                recv_sem=ship_recv_sems.at[i],
                device_id={"stream": ahead},
                device_id_type=MESH,
            )
            for i, (source, target) in enumerate(
                (
                    (table, next_table),
                    (piece_rhs_pad.at[halves[0]], next_rhs[0]),
                    (piece_blocks.at[parts[0]], piece_flat.at[parts[0]]),
                    (piece_rhs_pad.at[halves[1]], next_rhs[1]),
                    (piece_blocks.at[parts[1]], piece_flat.at[parts[1]]),
                )
            )
        ]

    @pl.when(section > 0)
    def _():
        for copy in shipments():
            copy.start()

    def send_first(group):
        def fill(box, turn):
            for place in range(CAP):
                piece = own_slots[turn, group * CAP + place]
                box[group, turn, pl.ds(place * R, R), :] = piece_rhs_pad[piece]

        def send(turn, device):
            fill(first_box, turn)
            pltpu.make_async_remote_copy(
                src_ref=first_box.at[group, turn],
                dst_ref=inbox.at[group, turn],
                send_sem=first_sems.at[group],
                recv_sem=inbox_sems.at[group, lax.div(turn, near)],
                device_id={"span": device},
                device_id_type=MESH,
            ).start()

        fill(inbox, span - 1)
        for_others(send)

    @pl.when(is_first)
    def _():
        pltpu.make_async_copy(table, own_slots, table_sems.at[0]).wait()
        send_first(0)

    def send_index(turn, device):
        pltpu.make_async_remote_copy(
            src_ref=index_out.at[turn],
            dst_ref=index_in.at[turn],
            send_sem=index_sems.at[0],
            recv_sem=index_sems.at[1],
            device_id={"span": device},
            device_id_type=MESH,
        ).start()

    index_in[span - 1] = index_out[span - 1]
    for_others(send_index)

    @pl.when(is_first)
    def _():
        send_first(1)

    @pl.when(jnp.logical_not(is_last))
    def _():
        whole_wait(next_table, ship_recv_sems.at[0])
        to_slots = pltpu.make_async_copy(next_table, slots_next, table_sems.at[1])
        to_slots.start()
        to_slots.wait()

    def couple(group):
        base = group * slot_grp
        start, count = (0, FIRST_ROWS) if group == 0 else (FIRST_ROWS, slots - FIRST_ROWS)
        whole_wait(next_rhs[group], ship_recv_sems.at[2 * group + 1])
        whole_wait(piece_flat.at[parts[group]], ship_recv_sems.at[2 * group + 2])
        unfolded(piece_flat, 0, start, count)

        @pl.loop(0, slot_grp // 8)
        def _(index):
            for j in range(8):
                block = base + index * 8 + j
                cell = group * cell_grp + slots_next[0, UP_LANE + block]
                coupling[block] = times_transposed(
                    inverse_t[cell], matrix(block).astype(jnp.bfloat16)
                ).astype(jnp.bfloat16)

    whole_wait(index_in.at[others], index_sems.at[1])
    row = lax.broadcasted_iota(jnp.int32, (cell_grp * R, LANES), 0)
    column = lax.broadcasted_iota(jnp.int32, (cell_grp * R, LANES), 1)
    same_side = row % R == column % R
    for group in range(GROUPS):
        for part in range(span // BLOCK):
            named = index_in[BLOCK * part, pl.ds(group, 1), :]
            for j in range(1, BLOCK):
                named = named + index_in[BLOCK * part + j, pl.ds(group, 1), :]
            hit = same_side & (row // R + 1 == named)
            half, place = divmod(part * BLOCK, near)
            selector[group, half, :, pl.ds(place * MSG, LANES)] = hit.astype(jnp.bfloat16)

    @pl.when(jnp.logical_not(is_last))
    def _():
        couple(0)

    is_late = section <= 1

    @pl.when(jnp.logical_not(is_last | is_late))
    def _():
        couple(1)

    def downstream(group, half):
        cells_of = pl.ds(half * HALF, HALF)
        return pltpu.make_async_remote_copy(
            src_ref=sent.at[group, cells_of],
            dst_ref=arrived[group].at[cells_of],
            send_sem=sent_sems.at[group],
            recv_sem=arrived_sems.at[group],
            device_id={"stream": after},
            device_id_type=MESH,
        )

    def own_terms(group):
        @pl.when(is_first)
        def _():
            owned[group] = rhs_pad[pl.ds(group * cell_grp, cell_grp)].astype(jnp.float32)

        @pl.when(section > 0)
        def _():
            whole_wait(arrived[group], arrived_sems.at[group])

            @pl.loop(0, cell_grp // 7)
            def _(index):
                for j in range(7):
                    cell = index * 7 + j
                    whole = group * cell_grp + cell
                    total = rhs_pad[whole].astype(jnp.float32)
                    states = jnp.concatenate(
                        [arrived[group][up_cells[face, whole]] for face in range(2)], axis=1
                    )
                    total = total - jnp.dot(
                        states, face_t[whole], preferred_element_type=jnp.float32
                    )
                    owned[group, cell] = total

    def merge(group):
        total = owned[group]
        for half, part in ((1, pl.ds(near, near)), (0, pl.ds(0, near))):

            @pl.when(is_first)
            def _():
                known = pl.ds(near, near - 1) if half else part
                whole_wait(inbox.at[group, known], inbox_sems.at[group, half])

            @pl.when(section > 0)
            def _():
                whole_wait(inbox.at[group, part], inbox_sems.at[group, half])

            messages = inbox[group, part].reshape(near * MSG, LANES)
            summed = jnp.dot(
                selector[group, half], messages, preferred_element_type=jnp.float32
            ).reshape(cell_grp, R, LANES)
            if half:
                owned[group] = total + summed
            else:
                merged[group] = (owned[group] + summed).astype(jnp.bfloat16)

    def send_partials(group, first, last):
        @pl.loop(first // places, last // places)
        def _(pair):
            for j in range(places):
                turn = pair * places + j
                for place in range(CAP):
                    column = group * CAP + place
                    piece = slots_next[turn, column]
                    state = merged[group, slots_next[turn, GROUPS * CAP + column]]
                    term = next_rhs[group][piece - group * slot_grp].astype(jnp.float32) - jnp.dot(
                        state, coupling[piece], preferred_element_type=jnp.float32
                    )
                    outbox[group, turn, pl.ds(place * R, R), :] = term.astype(jnp.bfloat16)
                pltpu.make_async_remote_copy(
                    src_ref=outbox.at[group, turn],
                    dst_ref=inbox.at[group, turn],
                    send_sem=outbox_sems.at[group],
                    recv_sem=inbox_sems.at[group, first // near],
                    device_id={"stream": after, "span": peer_at(pair, j)},
                    device_id_type=MESH,
                ).start()

    def solve(group):
        for half in range(cell_grp // HALF):
            for j in range(HALF):
                cell = half * HALF + j
                sent[group, cell] = jnp.dot(
                    merged[group, cell],
                    inverse_t[group * cell_grp + cell],
                    preferred_element_type=jnp.float32,
                ).astype(jnp.bfloat16)

            @pl.when(jnp.logical_not(is_last))
            def _():
                downstream(group, half).start()

    for group in range(GROUPS):
        if group == 1:

            @pl.when(is_late)
            def _():
                couple(1)

        own_terms(group)
        merge(group)

        @pl.when(jnp.logical_not(is_last))
        def _():
            send_partials(group, 0, near)

        solve(group)

        @pl.when(jnp.logical_not(is_last))
        def _():
            send_partials(group, near, span)

    for group in range(GROUPS):
        out[pl.ds(group * cell_grp, cell_grp)] = sent[group, :, :, :U]

    whole_wait(index_out.at[others], index_sems.at[0])

    @pl.when(section > 0)
    def _():
        for copy in shipments():
            copy.wait_send()

    @pl.when(is_first)
    def _():
        for group in range(GROUPS):
            whole_wait(first_box.at[group, others], first_sems.at[group])

    @pl.when(jnp.logical_not(is_last))
    def _():
        for group in range(GROUPS):
            whole_wait(outbox.at[group], outbox_sems.at[group])
            whole_wait(sent.at[group], sent_sems.at[group])


def on_device(
    sizes,
    right_side,
    up_blocks,
    inverses,
    up_cells,
    piece_rhs,
    piece_blocks,
    piece_up,
    piece_owner,
    piece_cell,
):
    sections, span_x, span_y, cells, slots = sizes
    span = span_x * span_y
    cell_grp = cells // GROUPS
    vmem = pl.BlockSpec(memory_space=pltpu.VMEM)
    smem = pl.BlockSpec(memory_space=pltpu.SMEM)
    bf16 = jnp.bfloat16
    states = pl.pallas_call(
        functools.partial(section_kernel, sizes),
        out_shape=jax.ShapeDtypeStruct((cells, R, U), bf16),
        in_specs=[smem] + [vmem] * 5 + [pl.BlockSpec(memory_space=pl.ANY)] * 3,
        out_specs=vmem,
        scratch_shapes=[
            pltpu.VMEM((cells, 2 * U * U), bf16),
            pltpu.VMEM((cells, U * U), bf16),
            pltpu.VMEM((slots, U * U), bf16),
            pltpu.VMEM((cells * STRIDE, LANES), jnp.float32),
            pltpu.VMEM((cells, 2 * LANES, LANES), bf16),
            pltpu.VMEM((cells, LANES, LANES), bf16),
            pltpu.VMEM((cells, R, LANES), bf16),
            pltpu.VMEM((slots, R, LANES), bf16),
            pltpu.VMEM((slots // GROUPS, R, LANES), bf16),
            pltpu.VMEM((slots // GROUPS, R, LANES), bf16),
            pltpu.VMEM((slots, LANES, LANES), bf16),
            pltpu.VMEM((span, LANES), jnp.int32),
            pltpu.VMEM((span, LANES), jnp.int32),
            pltpu.SMEM((span, LANES), jnp.int32),
            pltpu.SMEM((span, LANES), jnp.int32),
            pltpu.VMEM((span, GROUPS, LANES), jnp.int32),
            pltpu.VMEM((span, GROUPS, LANES), jnp.int32),
            pltpu.VMEM((GROUPS, 2, cell_grp * R, span // 2 * MSG), bf16),
            pltpu.VMEM((GROUPS, span, MSG, LANES), bf16),
            pltpu.VMEM((GROUPS, span, MSG, LANES), bf16),
            pltpu.VMEM((GROUPS, span, MSG, LANES), bf16),
            pltpu.VMEM((cell_grp, R, LANES), bf16),
            pltpu.VMEM((cell_grp, R, LANES), bf16),
            pltpu.VMEM((GROUPS, cell_grp, R, LANES), bf16),
            pltpu.VMEM((GROUPS, cell_grp, R, LANES), jnp.float32),
            pltpu.VMEM((GROUPS, cell_grp, R, LANES), bf16),
            pltpu.SemaphoreType.DMA((2,)),
            pltpu.SemaphoreType.DMA((2,)),
            pltpu.SemaphoreType.DMA((5,)),
            pltpu.SemaphoreType.DMA((5,)),
            pltpu.SemaphoreType.DMA((2,)),
            pltpu.SemaphoreType.DMA((GROUPS,)),
            pltpu.SemaphoreType.DMA((GROUPS,)),
            pltpu.SemaphoreType.DMA((GROUPS, 2)),
            pltpu.SemaphoreType.DMA((GROUPS,)),
            pltpu.SemaphoreType.DMA((GROUPS,)),
        ],
        compiler_params=pltpu.CompilerParams(
            collective_id=0, has_side_effects=True, vmem_limit_bytes=48 * 1024 * 1024
        ),
    )(
        up_cells[0].T,
        piece_owner.reshape(1, slots),
        piece_cell.reshape(1, slots),
        piece_up.reshape(1, slots),
        right_side.reshape(cells, U, R).swapaxes(1, 2),
        piece_rhs.reshape(slots, U, R).swapaxes(1, 2),
        up_blocks.reshape(cells, 2 * U * U),
        inverses.reshape(cells, U * U),
        piece_blocks.reshape(slots, U * U),
    )
    return states.swapaxes(1, 2).reshape(1, cells, U * R)


def solution(mesh):
    sections, span = mesh.shape["stream"], mesh.shape["span"]
    span_x = 4 if span == 32 else 2
    sizes = (sections, span_x, span // span_x, 56, 48)
    in_specs = (
        P("stream", "span", None),
        P("stream", "span", None),
        P("stream", "span", None),
        P("stream", "span", None),
        P("stream", "span", None),
        P("stream", "span", None),
        P("stream", "span"),
        P("stream", "span", None),
        P("stream", "span"),
    )
    out_specs = P("stream", "span", None)
    return jax.shard_map(
        functools.partial(on_device, sizes),
        mesh=mesh,
        in_specs=in_specs,
        out_specs=out_specs,
        check_vma=False,
    )
```

```python
import functools

import jax
import jax.numpy as jnp
from jax import lax
from jax.experimental import pallas as pl
from jax.experimental.pallas import tpu as pltpu
from jax.sharding import PartitionSpec as P

U = 100
R = 16
LANES = 128
GROUPS = 2
CAP = 2
MSG = CAP * R
BLOCK = 4
HALF = 14
UP_LANE = 64
STRIDE = 136
FOLD = 2048
FIRST_ROWS = 32
MESH = pl.DeviceIdType.MESH


def times_transposed(states, block):
    return lax.dot_general(
        states, block, (((1,), (1,)), ((), ())), preferred_element_type=jnp.float32
    )


def section_kernel(
    sizes,
    up_cells,
    owner_row,
    cell_row,
    up_row,
    right_side,
    piece_rhs,
    up_blocks,
    inverses,
    piece_blocks,
    out,
    face_flat,
    inverse_flat,
    piece_flat,
    spread,
    face_t,
    inverse_t,
    rhs_pad,
    piece_rhs_pad,
    next_rhs_0,
    next_rhs_1,
    coupling,
    table,
    next_table,
    own_slots,
    slots_next,
    index_out,
    index_in,
    selector,
    first_box,
    outbox,
    inbox,
    arrived_0,
    arrived_1,
    sent,
    owned,
    merged,
    load_sems,
    table_sems,
    ship_sems,
    ship_recv_sems,
    index_sems,
    first_sems,
    outbox_sems,
    inbox_sems,
    sent_sems,
    arrived_sems,
):
    sections, span_x, span_y, cells, slots = sizes
    span = span_x * span_y
    cell_grp, slot_grp = cells // GROUPS, slots // GROUPS
    section = lax.axis_index("stream")
    me = lax.axis_index("span")
    me_x, me_y = lax.div(me, span_y), lax.rem(me, span_y)
    after, ahead = lax.rem(section + 1, sections), lax.rem(section + sections - 1, sections)
    arrived = (arrived_0, arrived_1)
    next_rhs = (next_rhs_0, next_rhs_1)
    near = span // 2
    others = pl.ds(0, span - 1)
    is_first, is_last = section == 0, section == sections - 1

    order_x = sorted(range(span_x), key=lambda x: -min(x, span_x - x))

    def peer(turn):
        pair, place = turn // (2 * span_x), turn % span_x
        upper = turn // span_x % 2 == 0
        y = jnp.where(upper, span_y // 2 + pair, span_y // 2 - 1 - pair)
        x = sum(order_x[i] * jnp.where(place == i, 1, 0) for i in range(span_x))
        return (me_x + x) % span_x * span_y + (me_y + y) % span_y

    pairs, places = span_y // 2, 2 * span_x
    row_of = [lax.rem(me_x + x, span_x) * span_y for x in order_x]

    def peer_at(pair, place):
        y = span_y // 2 + pair if place < span_x else span_y // 2 - 1 - pair
        return row_of[place % span_x] + lax.rem(me_y + y, span_y)

    def for_others(act):
        @pl.loop(0, pairs)
        def _(pair):
            for place in range(places - 1):
                act(pair * places + place, peer_at(pair, place))

            @pl.when(pair < pairs - 1)
            def _():
                act(pair * places + places - 1, peer_at(pair, places - 1))

    def whole_wait(ref, sem):
        pltpu.make_async_copy(ref, ref, sem).wait()

    loads = [
        pltpu.make_async_copy(inverses, inverse_flat, load_sems.at[0]),
        pltpu.make_async_copy(up_blocks, face_flat, load_sems.at[1]),
    ]
    for load in loads:
        load.start()

    barrier = pltpu.get_barrier_semaphore()

    def greet(turn, device):
        pl.semaphore_signal(barrier, inc=1, device_id={"span": device}, device_id_type=MESH)

    @pl.loop(0, pairs)
    def _(pair):
        for place in range(places):
            pl.semaphore_signal(
                barrier,
                inc=1,
                device_id={"stream": ahead, "span": peer_at(pair, place)},
                device_id_type=MESH,
            )

    for_others(greet)
    pl.semaphore_signal(barrier, inc=1, device_id={"stream": after}, device_id_type=MESH)

    turn_col = lax.broadcasted_iota(jnp.int32, (span, slots), 0)
    slot_lane = lax.broadcasted_iota(jnp.int32, (span, slots), 1)
    match = owner_row[...] == peer(turn_col)
    lane = lax.broadcasted_iota(jnp.int32, (span, LANES), 1)
    mine = lane // MSG == lax.broadcasted_iota(jnp.int32, (span, LANES), 0) % BLOCK
    slot_values = jnp.zeros((span, LANES), jnp.int32)
    for group in range(GROUPS):
        indices = jnp.zeros((span, LANES), jnp.int32)
        named = match & (slot_lane // slot_grp == group)
        lowest = jnp.min(jnp.where(named, slot_lane, slots), axis=1, keepdims=True)
        highest = jnp.max(jnp.where(named, slot_lane, -1), axis=1, keepdims=True)
        found = (highest >= lowest, highest > lowest)
        for place, piece in enumerate((lowest, highest)):
            chosen = (slot_lane == piece) & found[place]
            piece = jnp.where(found[place], piece, group * slot_grp)
            target = jnp.sum(jnp.where(chosen, cell_row[...] + 1, 0), axis=1, keepdims=True)
            source = jnp.sum(jnp.where(chosen, up_row[...], 0), axis=1, keepdims=True)
            column = group * CAP + place
            slot_values = jnp.where(lane == column, piece, slot_values)
            slot_values = jnp.where(lane == GROUPS * CAP + column, source, slot_values)
            indices = jnp.where(mine & (lane // R % CAP == place), target, indices)
        index_out[:, group, :] = indices
    table[...] = slot_values
    table[:, UP_LANE : UP_LANE + slots] = jnp.broadcast_to(up_row[...], (span, slots))

    @pl.when(is_first)
    def _():
        pltpu.make_async_copy(table, own_slots, table_sems.at[0]).start()

    def folded(flat, target, count):
        for start in range(0, U * R, LANES):
            width = min(LANES, U * R - start)
            turned = flat[:, start : start + width].astype(jnp.float32).T
            spread[pl.ds(start, width), :count] = turned
        for side in range(R):
            rows = spread[pl.ds(side, U, stride=R), :].T
            spread[pl.ds(FOLD + side, count, stride=R), :U] = rows[:count]
        whole = spread[pl.ds(FOLD, count * R), :].astype(jnp.bfloat16)
        target[...] = whole.reshape(count, R, LANES)

    def unfolded(flat, offset, base, count):
        def tile(block, height):
            for i in range(U):
                start = offset + U * i
                rows = flat[pl.ds(block, height), start : start + U]
                spread[pl.ds(block * STRIDE + i, height, stride=STRIDE), :U] = rows.astype(
                    jnp.float32
                )

        @pl.loop(0, count // 16)
        def _(index):
            tile(pl.multiple_of(base + index * 16, 16), 16)

        if count % 16:
            tile(base + count // 16 * 16, count % 16)

    def matrix(block):
        return spread[pl.ds(block * STRIDE, LANES), :]

    def transposed(target, base, count):
        @pl.loop(0, count // BLOCK)
        def _(index):
            for j in range(BLOCK):
                block = index * BLOCK + j
                target[base + block] = matrix(block).T.astype(jnp.bfloat16)

    spread[...] = jnp.zeros_like(spread)
    folded(piece_rhs, piece_rhs_pad, slots)
    folded(right_side, rhs_pad, cells)
    spread[...] = jnp.zeros_like(spread)

    loads[0].wait()
    unfolded(inverse_flat, 0, 0, cells)
    transposed(inverse_t, 0, cells)

    loads[1].wait()

    @pl.when(section > 0)
    def _():
        for face in range(2):
            unfolded(face_flat, face * U * U, 0, cells)

            @pl.loop(0, cells // BLOCK)
            def _(index):
                for j in range(BLOCK):
                    cell = index * BLOCK + j
                    face_t[cell, pl.ds(face * LANES, LANES), :] = matrix(cell).T.astype(
                        jnp.bfloat16
                    )

    pl.semaphore_wait(barrier, 2 * span)

    halves = (pl.ds(0, slot_grp), pl.ds(slot_grp, slot_grp))
    parts = (pl.ds(0, FIRST_ROWS), pl.ds(FIRST_ROWS, slots - FIRST_ROWS))

    def shipments():
        return [
            pltpu.make_async_remote_copy(
                src_ref=source,
                dst_ref=target,
                send_sem=ship_sems.at[i],
                recv_sem=ship_recv_sems.at[i],
                device_id={"stream": ahead},
                device_id_type=MESH,
            )
            for i, (source, target) in enumerate(
                (
                    (table, next_table),
                    (piece_rhs_pad.at[halves[0]], next_rhs[0]),
                    (piece_blocks.at[parts[0]], piece_flat.at[parts[0]]),
                    (piece_rhs_pad.at[halves[1]], next_rhs[1]),
                    (piece_blocks.at[parts[1]], piece_flat.at[parts[1]]),
                )
            )
        ]

    @pl.when(section > 0)
    def _():
        for copy in shipments():
            copy.start()

    def send_first(group):
        def fill(box, turn):
            for place in range(CAP):
                piece = own_slots[turn, group * CAP + place]
                box[group, turn, pl.ds(place * R, R), :] = piece_rhs_pad[piece]

        def send(turn, device):
            fill(first_box, turn)
            pltpu.make_async_remote_copy(
                src_ref=first_box.at[group, turn],
                dst_ref=inbox.at[group, turn],
                send_sem=first_sems.at[group],
                recv_sem=inbox_sems.at[group, lax.div(turn, near)],
                device_id={"span": device},
                device_id_type=MESH,
            ).start()

        fill(inbox, span - 1)
        for_others(send)

    @pl.when(is_first)
    def _():
        pltpu.make_async_copy(table, own_slots, table_sems.at[0]).wait()
        send_first(0)

    def send_index(turn, device):
        pltpu.make_async_remote_copy(
            src_ref=index_out.at[turn],
            dst_ref=index_in.at[turn],
            send_sem=index_sems.at[0],
            recv_sem=index_sems.at[1],
            device_id={"span": device},
            device_id_type=MESH,
        ).start()

    index_in[span - 1] = index_out[span - 1]
    for_others(send_index)

    @pl.when(is_first)
    def _():
        send_first(1)

    @pl.when(jnp.logical_not(is_last))
    def _():
        whole_wait(next_table, ship_recv_sems.at[0])
        to_slots = pltpu.make_async_copy(next_table, slots_next, table_sems.at[1])
        to_slots.start()
        to_slots.wait()

    def couple(group):
        base = group * slot_grp
        start, count = (0, FIRST_ROWS) if group == 0 else (FIRST_ROWS, slots - FIRST_ROWS)
        whole_wait(next_rhs[group], ship_recv_sems.at[2 * group + 1])
        whole_wait(piece_flat.at[parts[group]], ship_recv_sems.at[2 * group + 2])
        unfolded(piece_flat, 0, start, count)

        @pl.loop(0, slot_grp // 8)
        def _(index):
            for j in range(8):
                block = base + index * 8 + j
                cell = group * cell_grp + slots_next[0, UP_LANE + block]
                coupling[block] = times_transposed(
                    inverse_t[cell], matrix(block).astype(jnp.bfloat16)
                ).astype(jnp.bfloat16)

    whole_wait(index_in.at[others], index_sems.at[1])
    row = lax.broadcasted_iota(jnp.int32, (cell_grp * R, LANES), 0)
    column = lax.broadcasted_iota(jnp.int32, (cell_grp * R, LANES), 1)
    same_side = row % R == column % R
    for group in range(GROUPS):
        for part in range(span // BLOCK):
            named = index_in[BLOCK * part, pl.ds(group, 1), :]
            for j in range(1, BLOCK):
                named = named + index_in[BLOCK * part + j, pl.ds(group, 1), :]
            hit = same_side & (row // R + 1 == named)
            half, place = divmod(part * BLOCK, near)
            selector[group, half, :, pl.ds(place * MSG, LANES)] = hit.astype(jnp.bfloat16)

    @pl.when(jnp.logical_not(is_last))
    def _():
        couple(0)

    is_late = section <= 1

    @pl.when(jnp.logical_not(is_last | is_late))
    def _():
        couple(1)

    def downstream(group, half):
        cells_of = pl.ds(half * HALF, HALF)
        return pltpu.make_async_remote_copy(
            src_ref=sent.at[group, cells_of],
            dst_ref=arrived[group].at[cells_of],
            send_sem=sent_sems.at[group],
            recv_sem=arrived_sems.at[group],
            device_id={"stream": after},
            device_id_type=MESH,
        )

    def own_terms(group):
        @pl.when(is_first)
        def _():
            owned[group] = rhs_pad[pl.ds(group * cell_grp, cell_grp)].astype(jnp.float32)

        @pl.when(section > 0)
        def _():
            whole_wait(arrived[group], arrived_sems.at[group])

            @pl.loop(0, cell_grp // 7)
            def _(index):
                for j in range(7):
                    cell = index * 7 + j
                    whole = group * cell_grp + cell
                    total = rhs_pad[whole].astype(jnp.float32)
                    states = jnp.concatenate(
                        [arrived[group][up_cells[face, whole]] for face in range(2)], axis=1
                    )
                    total = total - jnp.dot(
                        states, face_t[whole], preferred_element_type=jnp.float32
                    )
                    owned[group, cell] = total

    def merge(group):
        total = owned[group]
        for half, part in ((1, pl.ds(near, near)), (0, pl.ds(0, near))):

            @pl.when(is_first)
            def _():
                known = pl.ds(near, near - 1) if half else part
                whole_wait(inbox.at[group, known], inbox_sems.at[group, half])

            @pl.when(section > 0)
            def _():
                whole_wait(inbox.at[group, part], inbox_sems.at[group, half])

            messages = inbox[group, part].reshape(near * MSG, LANES)
            summed = jnp.dot(
                selector[group, half], messages, preferred_element_type=jnp.float32
            ).reshape(cell_grp, R, LANES)
            if half:
                owned[group] = total + summed
            else:
                merged[group] = (owned[group] + summed).astype(jnp.bfloat16)

    def send_partials(group, first, last):
        @pl.loop(first // places, last // places)
        def _(pair):
            for j in range(places):
                turn = pair * places + j
                for place in range(CAP):
                    column = group * CAP + place
                    piece = slots_next[turn, column]
                    state = merged[group, slots_next[turn, GROUPS * CAP + column]]
                    term = next_rhs[group][piece - group * slot_grp].astype(jnp.float32) - jnp.dot(
                        state, coupling[piece], preferred_element_type=jnp.float32
                    )
                    outbox[group, turn, pl.ds(place * R, R), :] = term.astype(jnp.bfloat16)
                pltpu.make_async_remote_copy(
                    src_ref=outbox.at[group, turn],
                    dst_ref=inbox.at[group, turn],
                    send_sem=outbox_sems.at[group],
                    recv_sem=inbox_sems.at[group, first // near],
                    device_id={"stream": after, "span": peer_at(pair, j)},
                    device_id_type=MESH,
                ).start()

    def solve(group):
        for half in range(cell_grp // HALF):
            for j in range(HALF):
                cell = half * HALF + j
                sent[group, cell] = jnp.dot(
                    merged[group, cell],
                    inverse_t[group * cell_grp + cell],
                    preferred_element_type=jnp.float32,
                ).astype(jnp.bfloat16)

            @pl.when(jnp.logical_not(is_last))
            def _():
                downstream(group, half).start()

    for group in range(GROUPS):
        if group == 1:

            @pl.when(is_late)
            def _():
                couple(1)

        own_terms(group)
        merge(group)

        @pl.when(jnp.logical_not(is_last))
        def _():
            send_partials(group, 0, near)

        solve(group)

        @pl.when(jnp.logical_not(is_last))
        def _():
            send_partials(group, near, span)

    for group in range(GROUPS):
        out[pl.ds(group * cell_grp, cell_grp)] = sent[group, :, :, :U]

    whole_wait(index_out.at[others], index_sems.at[0])

    @pl.when(section > 0)
    def _():
        for copy in shipments():
            copy.wait_send()

    @pl.when(is_first)
    def _():
        for group in range(GROUPS):
            whole_wait(first_box.at[group, others], first_sems.at[group])

    @pl.when(jnp.logical_not(is_last))
    def _():
        for group in range(GROUPS):
            whole_wait(outbox.at[group], outbox_sems.at[group])
            whole_wait(sent.at[group], sent_sems.at[group])


def on_device(
    sizes,
    right_side,
    up_blocks,
    inverses,
    up_cells,
    piece_rhs,
    piece_blocks,
    piece_up,
    piece_owner,
    piece_cell,
):
    sections, span_x, span_y, cells, slots = sizes
    span = span_x * span_y
    cell_grp = cells // GROUPS
    vmem = pl.BlockSpec(memory_space=pltpu.VMEM)
    smem = pl.BlockSpec(memory_space=pltpu.SMEM)
    bf16 = jnp.bfloat16
    states = pl.pallas_call(
        functools.partial(section_kernel, sizes),
        out_shape=jax.ShapeDtypeStruct((cells, R, U), bf16),
        in_specs=[smem] + [vmem] * 5 + [pl.BlockSpec(memory_space=pltpu.HBM)] * 3,
        out_specs=vmem,
        scratch_shapes=[
            pltpu.VMEM((cells, 2 * U * U), bf16),
            pltpu.VMEM((cells, U * U), bf16),
            pltpu.VMEM((slots, U * U), bf16),
            pltpu.VMEM((cells * STRIDE, LANES), jnp.float32),
            pltpu.VMEM((cells, 2 * LANES, LANES), bf16),
            pltpu.VMEM((cells, LANES, LANES), bf16),
            pltpu.VMEM((cells, R, LANES), bf16),
            pltpu.VMEM((slots, R, LANES), bf16),
            pltpu.VMEM((slots // GROUPS, R, LANES), bf16),
            pltpu.VMEM((slots // GROUPS, R, LANES), bf16),
            pltpu.VMEM((slots, LANES, LANES), bf16),
            pltpu.VMEM((span, LANES), jnp.int32),
            pltpu.VMEM((span, LANES), jnp.int32),
            pltpu.SMEM((span, LANES), jnp.int32),
            pltpu.SMEM((span, LANES), jnp.int32),
            pltpu.VMEM((span, GROUPS, LANES), jnp.int32),
            pltpu.VMEM((span, GROUPS, LANES), jnp.int32),
            pltpu.VMEM((GROUPS, 2, cell_grp * R, span // 2 * MSG), bf16),
            pltpu.VMEM((GROUPS, span, MSG, LANES), bf16),
            pltpu.VMEM((GROUPS, span, MSG, LANES), bf16),
            pltpu.VMEM((GROUPS, span, MSG, LANES), bf16),
            pltpu.VMEM((cell_grp, R, LANES), bf16),
            pltpu.VMEM((cell_grp, R, LANES), bf16),
            pltpu.VMEM((GROUPS, cell_grp, R, LANES), bf16),
            pltpu.VMEM((GROUPS, cell_grp, R, LANES), jnp.float32),
            pltpu.VMEM((GROUPS, cell_grp, R, LANES), bf16),
            pltpu.SemaphoreType.DMA((2,)),
            pltpu.SemaphoreType.DMA((2,)),
            pltpu.SemaphoreType.DMA((5,)),
            pltpu.SemaphoreType.DMA((5,)),
            pltpu.SemaphoreType.DMA((2,)),
            pltpu.SemaphoreType.DMA((GROUPS,)),
            pltpu.SemaphoreType.DMA((GROUPS,)),
            pltpu.SemaphoreType.DMA((GROUPS, 2)),
            pltpu.SemaphoreType.DMA((GROUPS,)),
            pltpu.SemaphoreType.DMA((GROUPS,)),
        ],
        compiler_params=pltpu.CompilerParams(
            collective_id=0, has_side_effects=True, vmem_limit_bytes=48 * 1024 * 1024
        ),
    )(
        up_cells[0].T,
        piece_owner.reshape(1, slots),
        piece_cell.reshape(1, slots),
        piece_up.reshape(1, slots),
        right_side.reshape(cells, U * R),
        piece_rhs.reshape(slots, U * R),
        up_blocks.reshape(cells, 2 * U * U),
        inverses.reshape(cells, U * U),
        piece_blocks.reshape(slots, U * U),
    )
    return states.swapaxes(1, 2).reshape(1, cells, U * R)


def solution(mesh):
    sections, span = mesh.shape["stream"], mesh.shape["span"]
    span_x = 4 if span == 32 else 2
    sizes = (sections, span_x, span // span_x, 56, 48)
    in_specs = (
        P("stream", "span", None),
        P("stream", "span", None),
        P("stream", "span", None),
        P("stream", "span", None),
        P("stream", "span", None),
        P("stream", "span", None),
        P("stream", "span"),
        P("stream", "span", None),
        P("stream", "span"),
    )
    out_specs = P("stream", "span", None)
    return jax.shard_map(
        functools.partial(on_device, sizes),
        mesh=mesh,
        in_specs=in_specs,
        out_specs=out_specs,
        check_vma=False,
    )
```
